256 devices in a mesh: role: 2 (over x_lo), dev: 64 (over y, x_hi, z), cores: 2 (over core).
Axes of the slice: x: 4 (x_hi: 2, x_lo: 2; x = x_hi * 2 + x_lo), y: 4, z: 8, core: 2. Of those that a mesh axis runs over, the one named last changes fastest.
Arguments:
- tokens: bfloat16 [4096, 3584], P(('role', 'dev', 'cores')), may hold values from -6 to 6
- norm_gain: float32 [3584], replicated, may hold values from 0.1 to 1.9
- routes: int32 [4096, 8], P(('role', 'dev', 'cores')), may hold values from 0 to 127, all different within a row; in each aligned block of 16 rows (0 to 15, 16 to 31, ...) at most 2 rows name the same one
- route_weight: float32 [4096, 8], P(('role', 'dev', 'cores')), may hold values from 0.05 to 0.35
- w_gate: bfloat16 [128, 3584, 1024], P(('role', 'dev'), None, 'cores'), may hold values from -0.09375 to 0.09375
- w_up: bfloat16 [128, 3584, 1024], P(('role', 'dev'), None, 'cores'), may hold values from -0.09375 to 0.09375
- w_down: bfloat16 [128, 1024, 3584], P(('role', 'dev'), 'cores'), may hold values from -0.1875 to 0.1875
- query_latent: bfloat16 [1024, 128, 512], P(('role', 'dev', 'cores')), may hold values from -21 to 21
- query_rope: bfloat16 [1024, 128, 64], P(('role', 'dev', 'cores')), may hold values from -6 to 6
- cache_latent: bfloat16 [1024, 256, 512], P(('role', 'dev', 'cores')), may hold values from -6 to 6
- cache_rope: bfloat16 [1024, 64, 256], P(('role', 'dev', 'cores')), may hold values from -6 to 6
- lengths: int32 [1024], P(('role', 'dev', 'cores')), may hold values from 1 to 256, 131072 in all
Outputs:
- layer_out: bfloat16 [4096, 3584], P(('role', 'dev', 'cores'))
- attention_latent: bfloat16 [1024, 128, 512], P(('role', 'dev', 'cores'))
The draws below stay inside these ranges and needn't reach their ends.
Inputs may be any that keep to these rules, and one draw needn't show every extreme that they name: `routes`: each token names 8 different experts; at most 2 of the 16 tokens of one device name the same expert.
All inputs are finite; a program needn't handle non-finite values. No bound on the sum of `lengths` on one device may be relied on, other than what follows from the above.
Results may differ from the reference program's by a relative error of at most 0.0048.
Values may be sent and summed in bfloat16 or wider, within the bound.
No kernel may reach another device: no remote copies, remote signals or barrier semaphores. Data moves between devices by JAX's collectives and lax.ppermute only.
A program may use at most 128 MiB of HBM per device.

```python
import math
import jax
import jax.numpy as jnp
import numpy as np
from jax import lax

D = 3584
HID = 1024
HEADS = 128
LAT = 512
ROPE = 64
TOPK = 8
TOK_DEV = 16
CTX = 256
EXPERTS = 128
CAP = 2
TOKENS = 4096
REQUESTS = 1024
DEVICES = 256


def draw_cache_latent(key, part):
    key = jax.random.fold_in(key, 3)
    values = jnp.clip(jax.random.normal(key, (REQUESTS, CTX, LAT), jnp.float32), -6.0, 6.0)
    return values.astype(jnp.bfloat16)


def draw_query_latent(key, part):
    key = jax.random.fold_in(key, 5)
    values = jnp.clip(jax.random.normal(key, (REQUESTS, HEADS, LAT), jnp.float32), -6.0, 6.0)
    return values.astype(jnp.bfloat16)


def steps_of(stream_key, extent, cuts, smallest, high):
    factor_of = 1.0
    for dim, parts in cuts:
        draws = jax.random.uniform(jax.random.fold_in(jax.random.fold_in(stream_key, 6), dim), (parts,), jnp.float32, smallest / len(cuts), high / len(cuts))
        factor_of = factor_of * jnp.repeat(jnp.exp(draws), extent[dim] // parts).reshape((-1,) + (1,) * (len(extent) - 1 - dim))
    return factor_of


def profile(number_of, total, reach, lean):
    weights = [(1 << 20) // math.isqrt(grade ** lean) + 1 for grade in range(2, number_of + 1)]
    surplus, holding = total - reach - (number_of - 1), [1] * (number_of - 1)
    while surplus > 0:
        movable = [i for i in range(number_of - 1) if holding[i] < reach]
        pool, left = sum([weights[i] for i in movable]), surplus
        for i in movable:
            more = min(reach - holding[i], max(1, left * weights[i] // pool), surplus)
            holding[i] = holding[i] + more
            surplus = surplus - more
    return np.array([reach] + holding)


def uneven(key, amount, total, most, slope):
    if amount == 2:
        one = jax.random.randint(key, (), max(1, total - most), min(most, total - 1) + 1)
        return jnp.stack([one, total - one])
    sizes = jnp.asarray(profile(amount, total, most, slope), jnp.int32)
    twos = (amount - 1) // 2
    source_of, receiver = sizes[1:1 + 2 * twos:2], sizes[2:2 + 2 * twos:2]
    room = jnp.minimum(source_of - 1, most - receiver)
    passed = jax.random.randint(jax.random.fold_in(key, 1), (twos,), 0, 1 << 20) % (room + 1)
    sizes = sizes.at[1:1 + 2 * twos:2].set(source_of - passed).at[2:2 + 2 * twos:2].set(receiver + passed)
    return sizes[jax.random.permutation(jax.random.fold_in(key, 2), amount)]


def assign_block(key, own, number, rows, number_of, top, reach, slope):
    ranking = jax.random.permutation(key, number_of)
    crowded, usual = portions_of(number_of, rows * top, reach, slope, True), portions_of(number_of, rows * top, reach, slope, False)
    places = jnp.arange(number_of)

    def named(sizes, turn):
        used = int((sizes > 0).sum())
        fixed = max(1, used // 4)
        shifted = fixed + (places - fixed + turn * (used - fixed)) % max(1, number_of - fixed)
        return jnp.zeros((number_of,), jnp.int32).at[ranking[jnp.where(places < fixed, places, shifted)]].set(jnp.asarray(sizes, jnp.int32))

    sizes = jnp.where(number % 4 == 0, named(crowded, number // 4), named(usual, number - number // 4 - 1))
    mixed = jax.random.permutation(jax.random.fold_in(own, 3), number_of)
    giver, taker = mixed[0:number_of // 2 * 2:2], mixed[1:number_of // 2 * 2:2]
    margin = jnp.minimum(sizes[giver] - 1, reach - sizes[taker]) // 2
    margin = jnp.where((giver == ranking[0]) | (taker == ranking[0]) | (sizes[taker] == 0), 0, jnp.maximum(margin, 0))
    shifted = jax.random.randint(jax.random.fold_in(own, 4), (number_of // 2,), 0, 1 << 20) % (margin + 1)
    sizes = sizes.at[giver].add(-shifted).at[taker].add(shifted)
    items = jnp.searchsorted(jnp.cumsum(sizes), jnp.arange(rows * top), side="right").astype(jnp.int32)
    table = items.reshape(top, rows).T
    table = table[jax.random.permutation(jax.random.fold_in(own, 1), rows)]
    turn = jax.random.randint(jax.random.fold_in(own, 2), (rows, 1), 0, top)
    return jnp.take_along_axis(table, (jnp.arange(top)[None, :] + turn) % top, axis=1)


def portions_of(count, total, limit, slope, full):
    loads = [(1 << 20) // math.isqrt(standing ** slope) + 1 for standing in range(1, count + 1)]
    largest = limit if full else min(limit, max(-(-total // count), total * loads[0] // sum(loads)))
    least = 1 if total - largest >= count - 1 else 0
    holding, spare = [largest] + [least] * (count - 1), total - largest - least * (count - 1)
    while spare > 0:
        free = [i for i in range(1, count) if holding[i] < largest] or [i for i in range(1, count) if holding[i] < limit]
        pool, left = sum([loads[i] for i in free]), spare
        for i in free:
            extra = min(limit - holding[i], max(1, left * loads[i] // pool), spare)
            holding[i] = holding[i] + extra
            spare = spare - extra
    return np.array(holding)


def scatter_about(key, shape, spread, most, pieces=(), kind=jnp.bfloat16):
    entries = spread * jax.random.normal(key, shape, jnp.float32)
    if pieces:
        entries = entries * steps_of(key, shape, pieces, -0.22, 0.18)
    return jnp.clip(entries, -most, most).astype(kind)


def setup_inputs(seed: int = 0) -> dict:
    keys = jax.random.split(jax.random.key(seed), 13)
    tokens = scatter_about(keys[0], (TOKENS, D), 1.0, 6.0, ((0, 256),))
    norm_gain = jnp.clip(1.0 + 0.18 * jax.random.normal(keys[1], (D,), jnp.float32), 0.1, 1.9)
    routes_keys = jax.random.split(jax.random.fold_in(keys[2], 1), TOKENS // TOK_DEV)
    routes_turns = jax.random.permutation(jax.random.fold_in(keys[2], 3), TOKENS // TOK_DEV)
    routes = jax.vmap(lambda own, number: assign_block(jax.random.fold_in(keys[2], 2), own, number, TOK_DEV, EXPERTS, TOPK, CAP, 2))(routes_keys, routes_turns).reshape((TOKENS, TOPK))
    route_weight = jnp.clip(0.05 + 0.29999999 * jax.random.uniform(keys[3], (TOKENS, TOPK), jnp.float32) ** steps_of(keys[3], (TOKENS, TOPK), ((0, 256),), -0.2, 0.2), 0.05, 0.35)
    w_gate = scatter_about(keys[4], (EXPERTS, D, HID), D ** -0.5, 0.09375, ((0, 128), (2, 2)))
    w_up = scatter_about(keys[5], (EXPERTS, D, HID), D ** -0.5, 0.09375, ((0, 128), (2, 2)))
    w_down = scatter_about(keys[6], (EXPERTS, HID, D), HID ** -0.5, 0.1875, ((0, 128), (1, 2)))
    query_latent = draw_query_latent(jax.random.fold_in(keys[12], 71), 0)
    query_rope = scatter_about(keys[8], (REQUESTS, HEADS, ROPE), 1.0, 6.0, ((0, 256),))
    cache_latent = draw_cache_latent(jax.random.fold_in(keys[12], 71), 0)
    cache_rope = scatter_about(keys[10], (REQUESTS, ROPE, CTX), 1.0, 6.0, ((0, 256),))
    lengths = uneven(keys[11], REQUESTS, REQUESTS * CTX // 2, CTX, 2).astype(jnp.int32)
    return dict(tokens=tokens, norm_gain=norm_gain, routes=routes, route_weight=route_weight, w_gate=w_gate, w_up=w_up, w_down=w_down, query_latent=query_latent, query_rope=query_rope, cache_latent=cache_latent, cache_rope=cache_rope, lengths=lengths)


score_scale = 192.0 ** (-0.5)
epsilon = 1e-06

def normalize(tokens, norm_gain):
    widened = tokens.astype(jnp.float32)
    inverse = lax.rsqrt(lax.optimization_barrier(jnp.mean(widened * widened, axis=-1, keepdims=True)) + epsilon)
    return (widened * inverse * norm_gain).astype(jnp.bfloat16)

def expert_block(selected, gate_matrix, up_matrix, down_matrix):
    gate_proj = jnp.dot(selected, gate_matrix, preferred_element_type=jnp.float32)
    up_proj = jnp.dot(selected, up_matrix, preferred_element_type=jnp.float32)
    hidden = (jax.nn.silu(gate_proj) * up_proj).astype(jnp.bfloat16)
    half_width = hidden.shape[1] // 2
    summed = jnp.zeros((selected.shape[0], down_matrix.shape[1]), jnp.float32)
    for portion in range(2):
        partial_value = jnp.dot(hidden[:, portion * half_width:(portion + 1) * half_width], down_matrix[portion * half_width:(portion + 1) * half_width], preferred_element_type=jnp.float32)
        summed = summed + lax.optimization_barrier(partial_value.astype(jnp.bfloat16)).astype(jnp.float32)
    return summed.astype(jnp.bfloat16)

def attend(query_latent, query_rope, cache_latent, cache_rope, length):
    scores = jnp.dot(query_latent, cache_latent.T, preferred_element_type=jnp.float32)
    scores = (scores + jnp.dot(query_rope, cache_rope, preferred_element_type=jnp.float32)) * score_scale
    in_range = jnp.arange(cache_latent.shape[0], dtype=jnp.int32) < length
    scores = jnp.where(in_range[None, :], scores, -1e+30)
    highest = lax.optimization_barrier(jnp.max(scores, axis=1, keepdims=True))
    weights = jnp.exp(scores - highest)
    probabilities = (weights / lax.optimization_barrier(jnp.sum(weights, axis=1, keepdims=True))).astype(jnp.bfloat16)
    return jnp.dot(probabilities, cache_latent, preferred_element_type=jnp.float32).astype(jnp.bfloat16)

def reference(tokens, norm_gain, routes, route_weight, w_gate, w_up, w_down, query_latent, query_rope, cache_latent, cache_rope, lengths):
    normed = normalize(tokens, norm_gain)
    expert_bound = CAP * DEVICES
    block_size = 128 if expert_bound % 128 == 0 else expert_bound

    def one_expert(combined, expert):
        chosen_mask = routes == expert
        weight = lax.optimization_barrier(jnp.sum(jnp.where(chosen_mask, route_weight, 0.0), axis=1))
        routed = jnp.any(chosen_mask, axis=1)
        routed_count = jnp.sum(routed.astype(jnp.int32))
        position = jnp.nonzero(routed, size=expert_bound, fill_value=0)[0].astype(jnp.int32)
        selected = normed[position]
        gate_matrix = w_gate[expert]
        up_matrix = w_up[expert]
        down_matrix = w_down[expert]
        outputs = []
        for start in range(0, expert_bound, block_size):
            block_rows = selected[start:start + block_size]

            def compute_block(operand):
                return expert_block(operand, gate_matrix, up_matrix, down_matrix)

            def zero_block(operand):
                return jnp.zeros((block_size, D), jnp.bfloat16)
            outputs.append(lax.cond(routed_count > start, compute_block, zero_block, block_rows))
        expert_rows = jnp.concatenate(outputs, axis=0)
        live = jnp.arange(expert_bound, dtype=jnp.int32) < routed_count
        contribution = jnp.where(live[:, None], weight[position][:, None] * expert_rows.astype(jnp.float32), 0.0)
        return (combined.at[position].add(contribution), None)
    combined, _ = lax.scan(one_expert, jnp.zeros((TOKENS, D), jnp.float32), jnp.arange(EXPERTS, dtype=jnp.int32))
    layer_out = (tokens.astype(jnp.float32) + combined).astype(jnp.bfloat16)
    attention_latent = lax.map(lambda request: attend(*request), (query_latent, query_rope, cache_latent, cache_rope, lengths))
    return (layer_out, attention_latent)
```

```python
import functools
import jax
import jax.numpy as jnp
from jax import lax
from jax.experimental import pallas as pl
from jax.experimental.pallas import tpu as pltpu
from jax.sharding import Mesh, PartitionSpec as P

score_scale = 192.0 ** (-0.5)
epsilon = 1e-06
PLANE = ("xl", "y", "xh")
EXPERT = ("xl", "y", "xh", "z")
ALL = ("xl", "y", "xh", "z", "c")
TAIL = 128
VMEM_LIMIT = 56 * 1024 * 1024


def attention(query_latent, query_rope, cache_latent, cache_rope, lengths):
    scores = jnp.einsum(
        "rhl,rpl->rhp", query_latent, cache_latent, preferred_element_type=jnp.float32
    )
    scores = (
        scores
        + jnp.einsum("rhk,rkp->rhp", query_rope, cache_rope, preferred_element_type=jnp.float32)
    ) * score_scale
    in_range = jnp.arange(cache_latent.shape[1], dtype=jnp.int32)[None, :] < lengths[:, None]
    scores = jnp.where(in_range[:, None, :], scores, -1e30)
    highest = jnp.max(scores, axis=2, keepdims=True)
    weights = jnp.exp(scores - highest)
    probabilities = (weights / jnp.sum(weights, axis=2, keepdims=True)).astype(jnp.bfloat16)
    return jnp.einsum(
        "rhp,rpl->rhl", probabilities, cache_latent, preferred_element_type=jnp.float32
    ).astype(jnp.bfloat16)


def call(kernel, out_shape, *operands, flops=0, scratch=()):
    moved = sum(x.size * x.dtype.itemsize for x in operands) + sum(
        x.size * x.dtype.itemsize for x in jax.tree.leaves(out_shape)
    )
    return pl.pallas_call(
        kernel,
        out_shape=out_shape,
        scratch_shapes=scratch,
        compiler_params=pltpu.CompilerParams(vmem_limit_bytes=VMEM_LIMIT),
        cost_estimate=pl.CostEstimate(flops=flops, bytes_accessed=moved, transcendentals=0),
    )(*operands)


def shape(*dims, dtype=jnp.bfloat16):
    return jax.ShapeDtypeStruct(dims, dtype)


def norm_kernel(tokens, gain, tail, packed):
    width = tokens.shape[1]
    widened = tokens[...].astype(jnp.float32)
    inverse = lax.rsqrt(jnp.mean(widened * widened, axis=1, keepdims=True) + epsilon)
    packed[:, :width] = (widened * inverse * gain[...]).astype(jnp.bfloat16)
    packed[:, width:] = tail[...]


def dispatch_kernel(top, own, *refs):
    blocks, (outgoing, scale) = refs[:-2], refs[-2:]
    count = blocks[0].shape[0]
    gathered = count * len(blocks)
    places = own.shape[1]
    width = outgoing.shape[1]
    info = jnp.concatenate([b[:, width:] for b in blocks], axis=0).astype(jnp.float32)
    experts = own[...]
    names = jnp.zeros((gathered, places), jnp.float32)
    weight = jnp.zeros((gathered, places), jnp.float32)
    for k in range(top):
        match = info[:, k : k + 1] == experts
        share = (
            info[:, top + k : top + k + 1]
            + info[:, 2 * top + k : 2 * top + k + 1]
            + info[:, 3 * top + k : 3 * top + k + 1]
        )
        names = jnp.where(match, 1.0, names)
        weight = weight + jnp.where(match, share, 0.0)
    row = lax.broadcasted_iota(jnp.int32, (gathered, gathered), 0)
    column = lax.broadcasted_iota(jnp.int32, (gathered, gathered), 1)
    before = jnp.where((column < row) & (column // count == row // count), 1.0, 0.0)
    rank = jnp.dot(
        before.astype(jnp.bfloat16), names.astype(jnp.bfloat16), preferred_element_type=jnp.float32
    )
    token = lax.broadcasted_iota(jnp.int32, (gathered, places), 0)
    slot = lax.broadcasted_iota(jnp.int32, (gathered, places), 1) % (2 * len(blocks))
    here = (names > 0.0) & ((token // count) * 2 + rank.astype(jnp.int32) == slot)
    scale[...] = jnp.where(here, weight, 0.0)
    place = jnp.where(here, 1.0, 0.0).astype(jnp.bfloat16)
    step = 512
    for start in range(0, width, step):
        rows = jnp.concatenate([b[:, start : start + step] for b in blocks], axis=0)
        outgoing[:, start : start + step] = lax.dot_general(
            place, rows, (((0,), (0,)), ((), ())), preferred_element_type=jnp.float32
        ).astype(jnp.bfloat16)


def combine_kernel(scale, returned, *blocks):
    count = blocks[0].shape[0]
    width = returned.shape[1]
    high = scale[...].astype(jnp.bfloat16)
    low = (scale[...] - high.astype(jnp.float32)).astype(jnp.bfloat16)
    step = 512
    for start in range(0, width, step):
        rows = returned[:, start : start + step]
        sums = jnp.dot(high, rows, preferred_element_type=jnp.float32) + jnp.dot(
            low, rows, preferred_element_type=jnp.float32
        )
        for i, block in enumerate(blocks):
            block[:, start : start + step] = sums[i * count : (i + 1) * count].astype(block.dtype)


def add_kernel(up2, up3, across, down2, down3, new_up2, new_down2):
    f32 = jnp.float32
    new_up2[...] = (
        up2[...].astype(f32) + up3[...].astype(f32) + across[...].astype(f32)
    ).astype(jnp.bfloat16)
    new_down2[...] = (down2[...].astype(f32) + down3[...].astype(f32)).astype(jnp.bfloat16)


def final_kernel(tokens, own, *refs):
    total = own[...]
    for part in refs[:-1]:
        total = total + part[...].astype(jnp.float32)
    refs[-1][...] = (tokens[...].astype(jnp.float32) + total).astype(jnp.bfloat16)


def expert_kernel(rows, *refs):
    weights, out, buffers, sems, total = refs[:6], refs[6], refs[7:13], refs[13], refs[14]
    tile = 256
    tiles = weights[0].shape[1] // tile
    copies = []
    for half in range(2):
        for t in range(tiles):
            group = []
            for m in range(3):
                cut = pl.ds(t * tile, tile)
                at = (cut, slice(None)) if m == 2 else (slice(None), cut)
                index = half * 3 + m
                copy = pltpu.make_async_copy(
                    weights[index].at[at], buffers[index].at[at], sems.at[index, t]
                )
                copy.start()
                group.append(copy)
            copies.append(group)
    x = rows[...]
    step = 512
    width = out.shape[1]
    for half in range(2):
        gate_buffer, up_buffer, down_buffer = buffers[half * 3 : half * 3 + 3]
        hidden = []
        for t in range(tiles):
            group = copies[half * tiles + t]
            cut = slice(t * tile, (t + 1) * tile)
            group[0].wait()
            gate = jnp.dot(x, gate_buffer[:, cut], preferred_element_type=jnp.float32)
            group[1].wait()
            up = jnp.dot(x, up_buffer[:, cut], preferred_element_type=jnp.float32)
            hidden.append((gate / (1.0 + jnp.exp(-gate)) * up).astype(jnp.bfloat16))
        for t in range(tiles):
            copies[half * tiles + t][2].wait()
        activation = jnp.concatenate(hidden, axis=1)
        for start in range(0, width, step):
            cut = slice(start, start + step)
            partial = jnp.dot(
                activation, down_buffer[:, cut], preferred_element_type=jnp.float32
            ).astype(jnp.bfloat16)
            if half == 0:
                total[:, cut] = partial
            else:
                out[:, cut] = (
                    total[:, cut].astype(jnp.float32) + partial.astype(jnp.float32)
                ).astype(jnp.bfloat16)


def experts(rows, weights):
    count, width = rows.shape
    any_space = pl.BlockSpec(memory_space=pl.ANY)
    flops = 2 * count * sum(w.size for w in weights)
    return pl.pallas_call(
        expert_kernel,
        out_shape=shape(count, width),
        in_specs=[pl.BlockSpec(memory_space=pltpu.VMEM)] + [any_space] * 6,
        out_specs=pl.BlockSpec(memory_space=pltpu.VMEM),
        scratch_shapes=[pltpu.VMEM(w.shape, w.dtype) for w in weights]
        + [pltpu.SemaphoreType.DMA((6, 2)), pltpu.VMEM((count, width), jnp.bfloat16)],
        compiler_params=pltpu.CompilerParams(vmem_limit_bytes=VMEM_LIMIT),
        cost_estimate=pl.CostEstimate(
            flops=flops, bytes_accessed=2 * sum(w.size for w in weights), transcendentals=0
        ),
    )(rows, *weights)


def from_line(rows, distance):
    planes = lax.axis_size("z")
    return lax.ppermute(rows, "z", [((i + distance) % planes, i) for i in range(planes)])


def per_device(
    tokens,
    norm_gain,
    routes,
    route_weight,
    w_gate,
    w_up,
    w_down,
    query_latent,
    query_rope,
    cache_latent,
    cache_rope,
    lengths,
):
    planes = lax.axis_size("z")
    places = lax.axis_size(PLANE)
    count, top = routes.shape
    width = tokens.shape[1]
    gathered = planes * count
    slots = 2 * planes

    high = route_weight.astype(jnp.bfloat16)
    rest = route_weight - high.astype(jnp.float32)
    middle = rest.astype(jnp.bfloat16)
    low = (rest - middle.astype(jnp.float32)).astype(jnp.bfloat16)
    tail = jnp.concatenate([routes.astype(jnp.bfloat16), high, middle, low], axis=1)
    tail = jnp.pad(tail, ((0, 0), (0, TAIL - 4 * top)))
    packed = call(norm_kernel, shape(count, width + TAIL), tokens, norm_gain[None], tail)

    up2, down2 = from_line(packed, 2), from_line(packed, -2)
    up1, down1 = from_line(packed, 1), from_line(packed, -1)
    across, up3, down3 = from_line(up2, 2), from_line(up2, 1), from_line(down2, -1)

    own = (
        (jnp.arange(places * slots, dtype=jnp.int32) // slots) * planes + lax.axis_index("z")
    ).astype(jnp.float32)[None]
    outgoing, scale = call(
        functools.partial(dispatch_kernel, top),
        (shape(places * slots, width), shape(gathered, places * slots, dtype=jnp.float32)),
        own,
        packed,
        up1,
        up2,
        up3,
        across,
        down3,
        down2,
        down1,
    )
    weights = (w_gate[0], w_up[0], w_down[0])
    *held, outgoing = lax.optimization_barrier((*weights, outgoing))
    far = [lax.ppermute(w, "c", [(0, 1), (1, 0)]) for w in held]
    arrived = lax.all_to_all(outgoing, PLANE, split_axis=0, concat_axis=0, tiled=True)
    result = experts(arrived, (*weights, *far))
    returned = lax.all_to_all(result, PLANE, split_axis=0, concat_axis=0, tiled=True)
    own, up1, up2, up3, across, down3, down2, down1 = call(
        combine_kernel,
        (shape(count, width, dtype=jnp.float32),) + (shape(count, width),) * (planes - 1),
        scale,
        returned,
    )
    across, up3, down3 = from_line(across, -2), from_line(up3, -1), from_line(down3, 1)
    up1, down1 = from_line(up1, -1), from_line(down1, 1)
    up2, down2 = call(
        add_kernel, (shape(count, width),) * 2, up2, up3, across, down2, down3
    )
    up2, down2 = from_line(up2, -2), from_line(down2, 2)
    layer_out = call(final_kernel, shape(count, width), tokens, own, up1, down1, up2, down2)
    return layer_out, attention(query_latent, query_rope, cache_latent, cache_rope, lengths)


def solution(mesh):
    split = Mesh(mesh.devices.reshape(2, 4, 2, 8, 2), ALL)
    return jax.shard_map(
        per_device,
        mesh=split,
        in_specs=(
            P(ALL, None),
            P(),
            P(ALL, None),
            P(ALL, None),
            P(EXPERT, None, "c"),
            P(EXPERT, None, "c"),
            P(EXPERT, "c", None),
            P(ALL, None, None),
            P(ALL, None, None),
            P(ALL, None, None),
            P(ALL, None, None),
            P(ALL),
        ),
        out_specs=(P(ALL, None), P(ALL, None, None)),
        check_vma=False,
    )
```

```python
import functools
import jax
import jax.numpy as jnp
from jax import lax
from jax.experimental import pallas as pl
from jax.experimental.pallas import tpu as pltpu
from jax.sharding import Mesh, PartitionSpec as P

score_scale = 192.0 ** (-0.5)
epsilon = 1e-06
PLANE = ("xl", "y", "xh")
EXPERT = ("xl", "y", "xh", "z")
ALL = ("xl", "y", "xh", "z", "c")
TAIL = 128
STEP = 512
MIB = 1024 * 1024


def attention(query_latent, query_rope, cache_latent, cache_rope, lengths):
    scores = jnp.einsum(
        "rhl,rpl->rhp", query_latent, cache_latent, preferred_element_type=jnp.float32
    )
    scores = (
        scores
        + jnp.einsum("rhk,rkp->rhp", query_rope, cache_rope, preferred_element_type=jnp.float32)
    ) * score_scale
    in_range = jnp.arange(cache_latent.shape[1], dtype=jnp.int32)[None, :] < lengths[:, None]
    scores = jnp.where(in_range[:, None, :], scores, -1e30)
    highest = jnp.max(scores, axis=2, keepdims=True)
    weights = jnp.exp(scores - highest)
    probabilities = (weights / jnp.sum(weights, axis=2, keepdims=True)).astype(jnp.bfloat16)
    return jnp.einsum(
        "rhp,rpl->rhl", probabilities, cache_latent, preferred_element_type=jnp.float32
    ).astype(jnp.bfloat16)


def call(kernel, out_shape, *operands, limit, flops=0, scratch=()):
    moved = sum(x.size * x.dtype.itemsize for x in operands) + sum(
        x.size * x.dtype.itemsize for x in jax.tree.leaves(out_shape)
    )
    return pl.pallas_call(
        kernel,
        out_shape=out_shape,
        scratch_shapes=scratch,
        compiler_params=pltpu.CompilerParams(vmem_limit_bytes=limit * MIB),
        cost_estimate=pl.CostEstimate(flops=flops, bytes_accessed=moved, transcendentals=0),
    )(*operands)


def shape(*dims, dtype=jnp.bfloat16):
    return jax.ShapeDtypeStruct(dims, dtype)


def in_hbm(x):
    return pltpu.with_memory_space_constraint(x, pltpu.HBM)


def norm_kernel(tokens_in, gain_in, routes_in, weight_in, packed, tokens, gain, routes, route_weight, sems):
    copies = [
        pltpu.make_async_copy(source, target, sems.at[i])
        for i, (source, target) in enumerate(
            (
                (routes_in, routes),
                (weight_in, route_weight),
                (tokens_in, tokens),
                (gain_in, gain.at[0]),
            )
        )
    ]
    for copy in copies:
        copy.start()
    width = tokens.shape[1]
    top = routes.shape[0]
    copies[0].wait()
    copies[1].wait()
    weight = route_weight[...]
    high = weight.astype(jnp.bfloat16).astype(jnp.float32)
    middle = (weight - high).astype(jnp.bfloat16).astype(jnp.float32)
    low = weight - high - middle
    columns = jnp.concatenate([routes[...].astype(jnp.float32), high, middle, low], axis=0)
    row = lax.broadcasted_iota(jnp.int32, (4 * top, TAIL), 0)
    column = lax.broadcasted_iota(jnp.int32, (4 * top, TAIL), 1)
    unit = jnp.where(row == column, 1.0, 0.0).astype(jnp.bfloat16)
    packed[:, width:] = lax.dot_general(
        columns.astype(jnp.bfloat16),
        unit,
        (((0,), (0,)), ((), ())),
        preferred_element_type=jnp.float32,
    ).astype(jnp.bfloat16)
    copies[2].wait()
    widened = tokens[...].astype(jnp.float32)
    inverse = lax.rsqrt(jnp.mean(widened * widened, axis=1, keepdims=True) + epsilon)
    copies[3].wait()
    packed[:, :width] = (widened * inverse * gain[...]).astype(jnp.bfloat16)


def normalize(tokens, gain, routes, route_weight):
    operands = (tokens, gain, routes.T, route_weight.T)
    return pl.pallas_call(
        norm_kernel,
        out_shape=shape(tokens.shape[0], tokens.shape[1] + TAIL),
        in_specs=[pl.BlockSpec(memory_space=pltpu.HBM)] * 4,
        scratch_shapes=[
            pltpu.VMEM(tokens.shape, tokens.dtype),
            pltpu.VMEM((1,) + gain.shape, gain.dtype),
            pltpu.VMEM(operands[2].shape, routes.dtype),
            pltpu.VMEM(operands[3].shape, route_weight.dtype),
            pltpu.SemaphoreType.DMA((4,)),
        ],
        compiler_params=pltpu.CompilerParams(vmem_limit_bytes=4 * MIB),
        cost_estimate=pl.CostEstimate(
            flops=4 * tokens.size, bytes_accessed=4 * tokens.size, transcendentals=0
        ),
    )(*(in_hbm(x) for x in operands))


def slots_of(info, experts, count, top):
    gathered, places = info.shape[0], experts.shape[1]
    names = jnp.zeros((gathered, places), jnp.float32)
    weight = jnp.zeros((gathered, places), jnp.float32)
    for k in range(top):
        match = info[:, k : k + 1] == experts
        share = (
            info[:, top + k : top + k + 1]
            + info[:, 2 * top + k : 2 * top + k + 1]
            + info[:, 3 * top + k : 3 * top + k + 1]
        )
        names = jnp.where(match, 1.0, names)
        weight = weight + jnp.where(match, share, 0.0)
    row = lax.broadcasted_iota(jnp.int32, (gathered, gathered), 0)
    column = lax.broadcasted_iota(jnp.int32, (gathered, gathered), 1)
    before = jnp.where((column < row) & (column // count == row // count), 1.0, 0.0)
    rank = jnp.dot(
        before.astype(jnp.bfloat16), names.astype(jnp.bfloat16), preferred_element_type=jnp.float32
    )
    token = lax.broadcasted_iota(jnp.int32, (gathered, places), 0)
    slot = lax.broadcasted_iota(jnp.int32, (gathered, places), 1) % (2 * gathered // count)
    here = (names > 0.0) & ((token // count) * 2 + rank.astype(jnp.int32) == slot)
    return jnp.where(here, 1.0, 0.0), jnp.where(here, weight, 0.0)


def dispatch_kernel(top, own, own_half, *refs):
    blocks, (outgoing, near_scale, far_scale, built, sems) = refs[:-5], refs[-5:]
    count = blocks[0].shape[0]
    half = count * len(blocks) // 2
    width = outgoing.shape[1]
    info = jnp.concatenate([b[:, width:] for b in blocks], axis=0).astype(jnp.float32)
    place, _ = slots_of(info, own[...], count, top)
    place = place.astype(jnp.bfloat16)
    copies = []
    for i, start in enumerate(range(0, width, STEP)):
        cut = pl.ds(start, STEP)
        rows = jnp.concatenate([b[:, start : start + STEP] for b in blocks], axis=0)
        built[:, cut] = lax.dot_general(
            place, rows, (((0,), (0,)), ((), ())), preferred_element_type=jnp.float32
        ).astype(jnp.bfloat16)
        copies.append(pltpu.make_async_copy(built.at[:, cut], outgoing.at[:, cut], sems.at[i]))
        copies[-1].start()
    _, near_scale[...] = slots_of(info[:half], own_half[...], count, top)
    _, far_scale[...] = slots_of(info[half:], own_half[...], count, top)
    for copy in copies:
        copy.wait()


def dispatch(top, rows, width, own, own_half, *blocks):
    gathered = blocks[0].shape[0] * len(blocks)
    any_vmem = pl.BlockSpec(memory_space=pltpu.VMEM)
    return pl.pallas_call(
        functools.partial(dispatch_kernel, top),
        out_shape=[pltpu.HBM((rows, width), jnp.bfloat16)]
        + [shape(gathered // 2, rows // 2, dtype=jnp.float32)] * 2,
        out_specs=[pl.BlockSpec(memory_space=pltpu.HBM), any_vmem, any_vmem],
        scratch_shapes=[
            pltpu.VMEM((rows, width), jnp.bfloat16),
            pltpu.SemaphoreType.DMA((width // STEP,)),
        ],
        compiler_params=pltpu.CompilerParams(vmem_limit_bytes=10 * MIB),
        cost_estimate=pl.CostEstimate(
            flops=2 * rows * gathered * width,
            bytes_accessed=4 * rows * width,
            transcendentals=0,
        ),
    )(own, own_half, *blocks)


def weighted(scale, rows):
    high = scale.astype(jnp.bfloat16)
    low = (scale - high.astype(jnp.float32)).astype(jnp.bfloat16)
    return jnp.dot(high, rows, preferred_element_type=jnp.float32) + jnp.dot(
        low, rows, preferred_element_type=jnp.float32
    )


def far_kernel(scale, returned, *blocks):
    count, width = blocks[0].shape
    step = 512
    for start in range(0, width, step):
        cut = slice(start, start + step)
        sums = weighted(scale[...], returned[:, cut])
        for i, block in enumerate(blocks):
            block[:, cut] = sums[i * count : (i + 1) * count].astype(block.dtype)


def near_kernel(scale, returned, up3, across, down3, down2_far, own, up1, down1, up2, down2):
    count, width = own.shape
    f32 = jnp.float32
    step = 512
    for start in range(0, width, step):
        cut = slice(start, start + step)
        sums = weighted(scale[...], returned[:, cut])
        own[:, cut] = sums[:count]
        up1[:, cut] = sums[count : 2 * count].astype(jnp.bfloat16)
        down1[:, cut] = sums[2 * count : 3 * count].astype(jnp.bfloat16)
        up2[:, cut] = (
            sums[3 * count :] + up3[:, cut].astype(f32) + across[:, cut].astype(f32)
        ).astype(jnp.bfloat16)
    down2[...] = (down2_far[...] + down3[...].astype(f32)).astype(jnp.bfloat16)


def final_kernel(tokens, own, *refs):
    total = own[...]
    for part in refs[:-1]:
        total = total + part[...].astype(jnp.float32)
    refs[-1][...] = (tokens[...].astype(jnp.float32) + total).astype(jnp.bfloat16)


def expert_kernel(rows, *refs):
    weights, (near, far), held = refs[:6], refs[6:8], refs[8:14]
    near_built, far_built, total, sems, out_sems = refs[14:]
    width = near.shape[1]
    copies = [pltpu.make_async_copy(weights[i], held[i], sems.at[i]) for i in range(6)]
    for copy in copies:
        copy.start()
    x = rows[...]
    sent = []
    for half in range(2):
        gate_copy, up_copy, down_copy = copies[3 * half : 3 * half + 3]
        gate_half, up_half, down_half = held[3 * half : 3 * half + 3]
        gate_copy.wait()
        gate = jnp.dot(x, gate_half[...], preferred_element_type=jnp.float32)
        up_copy.wait()
        up = jnp.dot(x, up_half[...], preferred_element_type=jnp.float32)
        activation = (gate / (1.0 + jnp.exp(-gate)) * up).astype(jnp.bfloat16)
        down_copy.wait()
        for i, start in enumerate(range(0, width, STEP)):
            cut = pl.ds(start, STEP)
            partial = jnp.dot(
                activation, down_half[:, cut], preferred_element_type=jnp.float32
            ).astype(jnp.bfloat16)
            if half == 0:
                total[:, cut] = partial
                continue
            sums = total[:, cut].astype(jnp.float32) + partial.astype(jnp.float32)
            sums = sums.reshape(-1, 2, 8, STEP)
            for j, (built, out) in enumerate(((near_built, near), (far_built, far))):
                built[:, cut] = sums[:, j].reshape(-1, STEP).astype(jnp.bfloat16)
                sent.append(
                    pltpu.make_async_copy(built.at[:, cut], out.at[:, cut], out_sems.at[j, i])
                )
                sent[-1].start()
    for copy in sent:
        copy.wait()


def experts(rows, weights):
    count, width = rows.shape
    hbm = pl.BlockSpec(memory_space=pltpu.HBM)
    half = (count // 2, width)
    return pl.pallas_call(
        expert_kernel,
        out_shape=[pltpu.HBM(half, rows.dtype)] * 2,
        in_specs=[pl.BlockSpec(memory_space=pltpu.VMEM)] + [hbm] * 6,
        out_specs=[hbm] * 2,
        scratch_shapes=[pltpu.VMEM(w.shape, w.dtype) for w in weights]
        + [pltpu.VMEM(half, rows.dtype)] * 2
        + [
            pltpu.VMEM(rows.shape, rows.dtype),
            pltpu.SemaphoreType.DMA((6,)),
            pltpu.SemaphoreType.DMA((2, width // STEP)),
        ],
        compiler_params=pltpu.CompilerParams(vmem_limit_bytes=40 * MIB),
        cost_estimate=pl.CostEstimate(
            flops=2 * count * sum(w.size for w in weights),
            bytes_accessed=2 * sum(w.size for w in weights),
            transcendentals=0,
        ),
    )(rows, *(in_hbm(w) for w in weights))


def from_line(rows, distance):
    planes = lax.axis_size("z")
    return lax.ppermute(rows, "z", [((i + distance) % planes, i) for i in range(planes)])


def per_device(
    tokens,
    norm_gain,
    routes,
    route_weight,
    w_gate,
    w_up,
    w_down,
    query_latent,
    query_rope,
    cache_latent,
    cache_rope,
    lengths,
):
    planes = lax.axis_size("z")
    places = lax.axis_size(PLANE)
    count, top = routes.shape
    width = tokens.shape[1]
    slots = 2 * planes
    rows = places * slots
    gathered = count * planes
    f32 = jnp.float32

    def to_plane(x):
        return lax.all_to_all(x, PLANE, split_axis=0, concat_axis=0, tiled=True)

    packed = normalize(tokens, norm_gain, routes, route_weight)
    weights = (w_gate[0], w_up[0], w_down[0])

    up2, down2 = from_line(packed, 2), from_line(packed, -2)
    up1, down1 = from_line(packed, 1), from_line(packed, -1)
    (up1, down1, up2, down2), held = lax.optimization_barrier(
        ((up1, down1, up2, down2), weights[1:])
    )
    across, up3, down3 = from_line(up2, 2), from_line(up2, 1), from_line(down2, -1)
    far_weights = [lax.ppermute(w, "c", [(0, 1), (1, 0)]) for w in (weights[0], *held)]

    own, own_half = (
        (
            (jnp.arange(places * n, dtype=jnp.int32) // n) * planes + lax.axis_index("z")
        ).astype(f32)[None]
        for n in (slots, slots // 2)
    )

    outgoing, near_scale, far_scale = dispatch(
        top, rows, width, own, own_half, packed, up1, down1, up2, down2, up3, across, down3
    )
    arrived = to_plane(outgoing)
    near_result, far_result = experts(arrived, (*weights, *far_weights))
    far_back = to_plane(far_result)
    far_back, near_result = lax.optimization_barrier((far_back, near_result))
    near_back = to_plane(near_result)
    flops = rows * gathered * width
    down2_far, up3, across, down3 = call(
        far_kernel,
        (shape(count, width, dtype=f32),) + (shape(count, width),) * 3,
        far_scale,
        far_back,
        limit=8,
        flops=flops,
    )
    across, up3, down3 = from_line(across, -2), from_line(up3, -1), from_line(down3, 1)
    own_sum, up1, down1, up2, down2 = call(
        near_kernel,
        (shape(count, width, dtype=f32),) + (shape(count, width),) * 4,
        near_scale,
        near_back,
        up3,
        across,
        down3,
        down2_far,
        limit=8,
        flops=flops,
    )
    up2, down2 = from_line(up2, -2), from_line(down2, 2)
    up1, down1 = from_line(up1, -1), from_line(down1, 1)
    layer_out = call(
        final_kernel, shape(count, width), tokens, own_sum, up1, down1, up2, down2, limit=4
    )
    return layer_out, attention(query_latent, query_rope, cache_latent, cache_rope, lengths)


def solution(mesh):
    split = Mesh(mesh.devices.reshape(2, 4, 2, 8, 2), ALL)
    return jax.shard_map(
        per_device,
        mesh=split,
        in_specs=(
            P(ALL, None),
            P(),
            P(ALL, None),
            P(ALL, None),
            P(EXPERT, None, "c"),
            P(EXPERT, None, "c"),
            P(EXPERT, "c", None),
            P(ALL, None, None),
            P(ALL, None, None),
            P(ALL, None, None),
            P(ALL, None, None),
            P(ALL),
        ),
        out_specs=(P(ALL, None), P(ALL, None, None)),
        check_vma=False,
    )
```

```python
import functools
import jax
import jax.numpy as jnp
from jax import lax
from jax.experimental import pallas as pl
from jax.experimental.pallas import tpu as pltpu
from jax.sharding import Mesh, PartitionSpec as P

score_scale = 192.0 ** (-0.5)
epsilon = 1e-06
PLANE = ("xl", "y", "xh")
EXPERT = ("xl", "y", "xh", "z")
ALL = ("xl", "y", "xh", "z", "c")
TAIL = 128
STEP = 512
MIB = 1024 * 1024


def attention_kernel(lengths, latent_in, rope_in, cache_in, cache_rope_in, out, *scratch):
    latent, rope, cache, cache_rope, built, sems, out_sems = scratch
    requests, positions = cache.shape[0], cache.shape[1]
    sources = (cache_in, latent_in, cache_rope_in, rope_in)
    targets = (cache, latent, cache_rope, rope)
    copies = [
        [
            pltpu.make_async_copy(source.at[r], target.at[r], sems.at[i, r])
            for i, (source, target) in enumerate(zip(sources, targets))
        ]
        for r in range(requests)
    ]
    for group in copies:
        for copy in group:
            copy.start()
    sent = []
    for r in range(requests):
        for copy in copies[r]:
            copy.wait()
        keys = cache[r]
        scores = lax.dot_general(
            latent[r], keys, (((1,), (1,)), ((), ())), preferred_element_type=jnp.float32
        )
        scores = (
            scores
            + lax.dot_general(
                rope[r], cache_rope[r], (((0,), (0,)), ((), ())), preferred_element_type=jnp.float32
            )
        ) * score_scale
        position = lax.broadcasted_iota(jnp.int32, scores.shape, 1)
        scores = jnp.where(position < lengths[r], scores, -1e30)
        weights = jnp.exp(scores - jnp.max(scores, axis=1, keepdims=True))
        probabilities = weights / jnp.sum(weights, axis=1, keepdims=True)
        built[r] = jnp.dot(
            probabilities.astype(jnp.bfloat16), keys, preferred_element_type=jnp.float32
        ).astype(jnp.bfloat16)
        sent.append(pltpu.make_async_copy(built.at[r], out.at[r], out_sems.at[r]))
        sent[-1].start()
    for copy in sent:
        copy.wait()


def attention(query_latent, query_rope, cache_latent, cache_rope, lengths):
    operands = (query_latent, jnp.swapaxes(query_rope, 1, 2), cache_latent, cache_rope)
    requests = lengths.shape[0]
    hbm = pl.BlockSpec(memory_space=pltpu.HBM)
    return pl.pallas_call(
        attention_kernel,
        out_shape=pltpu.HBM(query_latent.shape, query_latent.dtype),
        in_specs=[pl.BlockSpec(memory_space=pltpu.SMEM)] + [hbm] * 4,
        out_specs=hbm,
        scratch_shapes=[pltpu.VMEM(x.shape, x.dtype) for x in operands]
        + [
            pltpu.VMEM(query_latent.shape, query_latent.dtype),
            pltpu.SemaphoreType.DMA((4, requests)),
            pltpu.SemaphoreType.DMA((requests,)),
        ],
        compiler_params=pltpu.CompilerParams(vmem_limit_bytes=12 * MIB),
        cost_estimate=pl.CostEstimate(
            flops=4 * cache_latent.size * query_latent.shape[1],
            bytes_accessed=4 * cache_latent.size,
            transcendentals=0,
        ),
    )(lengths, *(in_hbm(x) for x in operands))


def call(kernel, out_shape, *operands, limit, flops=0, scratch=()):
    moved = sum(x.size * x.dtype.itemsize for x in operands) + sum(
        x.size * x.dtype.itemsize for x in jax.tree.leaves(out_shape)
    )
    return pl.pallas_call(
        kernel,
        out_shape=out_shape,
        scratch_shapes=scratch,
        compiler_params=pltpu.CompilerParams(vmem_limit_bytes=limit * MIB),
        cost_estimate=pl.CostEstimate(flops=flops, bytes_accessed=moved, transcendentals=0),
    )(*operands)


def shape(*dims, dtype=jnp.bfloat16):
    return jax.ShapeDtypeStruct(dims, dtype)


def in_hbm(x):
    return pltpu.with_memory_space_constraint(x, pltpu.HBM)


def norm_kernel(tokens_in, gain_in, routes_in, weight_in, packed, tokens, gain, routes, route_weight, sems):
    copies = [
        pltpu.make_async_copy(source, target, sems.at[i])
        for i, (source, target) in enumerate(
            (
                (routes_in, routes),
                (weight_in, route_weight),
                (tokens_in, tokens),
                (gain_in, gain.at[0]),
            )
        )
    ]
    for copy in copies:
        copy.start()
    width = tokens.shape[1]
    top = routes.shape[0]
    copies[0].wait()
    copies[1].wait()
    weight = route_weight[...]
    high = weight.astype(jnp.bfloat16).astype(jnp.float32)
    middle = (weight - high).astype(jnp.bfloat16).astype(jnp.float32)
    low = weight - high - middle
    columns = jnp.concatenate([routes[...].astype(jnp.float32), high, middle, low], axis=0)
    row = lax.broadcasted_iota(jnp.int32, (4 * top, TAIL), 0)
    column = lax.broadcasted_iota(jnp.int32, (4 * top, TAIL), 1)
    unit = jnp.where(row == column, 1.0, 0.0).astype(jnp.bfloat16)
    packed[:, width:] = lax.dot_general(
        columns.astype(jnp.bfloat16),
        unit,
        (((0,), (0,)), ((), ())),
        preferred_element_type=jnp.float32,
    ).astype(jnp.bfloat16)
    copies[2].wait()
    widened = tokens[...].astype(jnp.float32)
    inverse = lax.rsqrt(jnp.mean(widened * widened, axis=1, keepdims=True) + epsilon)
    copies[3].wait()
    packed[:, :width] = (widened * inverse * gain[...]).astype(jnp.bfloat16)


def normalize(tokens, gain, routes, route_weight):
    operands = (tokens, gain, routes.T, route_weight.T)
    return pl.pallas_call(
        norm_kernel,
        out_shape=shape(tokens.shape[0], tokens.shape[1] + TAIL),
        in_specs=[pl.BlockSpec(memory_space=pltpu.HBM)] * 4,
        scratch_shapes=[
            pltpu.VMEM(tokens.shape, tokens.dtype),
            pltpu.VMEM((1,) + gain.shape, gain.dtype),
            pltpu.VMEM(operands[2].shape, routes.dtype),
            pltpu.VMEM(operands[3].shape, route_weight.dtype),
            pltpu.SemaphoreType.DMA((4,)),
        ],
        compiler_params=pltpu.CompilerParams(vmem_limit_bytes=4 * MIB),
        cost_estimate=pl.CostEstimate(
            flops=4 * tokens.size, bytes_accessed=4 * tokens.size, transcendentals=0
        ),
    )(*(in_hbm(x) for x in operands))


def slots_of(info, experts, count, top):
    gathered, places = info.shape[0], experts.shape[1]
    names = jnp.zeros((gathered, places), jnp.float32)
    weight = jnp.zeros((gathered, places), jnp.float32)
    for k in range(top):
        match = info[:, k : k + 1] == experts
        share = (
            info[:, top + k : top + k + 1]
            + info[:, 2 * top + k : 2 * top + k + 1]
            + info[:, 3 * top + k : 3 * top + k + 1]
        )
        names = jnp.where(match, 1.0, names)
        weight = weight + jnp.where(match, share, 0.0)
    row = lax.broadcasted_iota(jnp.int32, (gathered, gathered), 0)
    column = lax.broadcasted_iota(jnp.int32, (gathered, gathered), 1)
    before = jnp.where((column < row) & (column // count == row // count), 1.0, 0.0)
    rank = jnp.dot(
        before.astype(jnp.bfloat16), names.astype(jnp.bfloat16), preferred_element_type=jnp.float32
    )
    token = lax.broadcasted_iota(jnp.int32, (gathered, places), 0)
    slot = lax.broadcasted_iota(jnp.int32, (gathered, places), 1) % (2 * gathered // count)
    here = (names > 0.0) & ((token // count) * 2 + rank.astype(jnp.int32) == slot)
    return jnp.where(here, 1.0, 0.0), jnp.where(here, weight, 0.0)


def dispatch_kernel(top, own, *refs):
    blocks, (outgoing, scale, built, sems) = refs[:-4], refs[-4:]
    count = blocks[0].shape[0]
    width = outgoing.shape[1]
    info = jnp.concatenate([b[:, width:] for b in blocks], axis=0).astype(jnp.float32)
    place, scale[...] = slots_of(info, own[...], count, top)
    place = place.astype(jnp.bfloat16)
    copies = []
    for i, start in enumerate(range(0, width, STEP)):
        cut = pl.ds(start, STEP)
        rows = jnp.concatenate([b[:, start : start + STEP] for b in blocks], axis=0)
        built[:, cut] = lax.dot_general(
            place, rows, (((0,), (0,)), ((), ())), preferred_element_type=jnp.float32
        ).astype(jnp.bfloat16)
        copies.append(pltpu.make_async_copy(built.at[:, cut], outgoing.at[:, cut], sems.at[i]))
        copies[-1].start()
    for copy in copies:
        copy.wait()


def dispatch(top, width, own, *blocks):
    gathered, rows = blocks[0].shape[0] * len(blocks), own.shape[1]
    return pl.pallas_call(
        functools.partial(dispatch_kernel, top),
        out_shape=[
            pltpu.HBM((rows, width), jnp.bfloat16),
            shape(gathered, rows, dtype=jnp.float32),
        ],
        out_specs=[pl.BlockSpec(memory_space=pltpu.HBM), pl.BlockSpec(memory_space=pltpu.VMEM)],
        scratch_shapes=[
            pltpu.VMEM((rows, width), jnp.bfloat16),
            pltpu.SemaphoreType.DMA((width // STEP,)),
        ],
        compiler_params=pltpu.CompilerParams(vmem_limit_bytes=8 * MIB),
        cost_estimate=pl.CostEstimate(
            flops=2 * rows * gathered * width,
            bytes_accessed=4 * rows * width,
            transcendentals=0,
        ),
    )(own, *blocks)


def weighted(scale, rows):
    high = scale.astype(jnp.bfloat16)
    low = (scale - high.astype(jnp.float32)).astype(jnp.bfloat16)
    return jnp.dot(high, rows, preferred_element_type=jnp.float32) + jnp.dot(
        low, rows, preferred_element_type=jnp.float32
    )


def far_kernel(scale, returned, *blocks):
    count, width = blocks[0].shape
    step = 512
    for start in range(0, width, step):
        cut = slice(start, start + step)
        sums = weighted(scale[...], returned[:, cut])
        for i, block in enumerate(blocks):
            block[:, cut] = sums[i * count : (i + 1) * count].astype(block.dtype)


def near_kernel(scale, returned, up3, across, down3, own, up1, up2, down2):
    count, width = own.shape
    f32 = jnp.float32
    for start in range(0, width, STEP):
        cut = slice(start, start + STEP)
        sums = weighted(scale[...], returned[:, cut])
        own[:, cut] = sums[:count]
        up1[:, cut] = sums[count : 2 * count].astype(jnp.bfloat16)
        up2[:, cut] = (
            sums[2 * count : 3 * count] + up3[:, cut].astype(f32) + across[:, cut].astype(f32)
        ).astype(jnp.bfloat16)
        down2[:, cut] = (sums[3 * count :] + down3[:, cut].astype(f32)).astype(jnp.bfloat16)


def final_kernel(tokens, own, *refs):
    total = own[...]
    for part in refs[:-1]:
        total = total + part[...].astype(jnp.float32)
    refs[-1][...] = (tokens[...].astype(jnp.float32) + total).astype(jnp.bfloat16)


def expert_kernel(near_rows, far_rows, *refs):
    weights, (near, far), held = refs[:6], refs[6:8], refs[8:14]
    near_built, far_built, total, sems, out_sems = refs[14:]
    count, width = near.shape
    copies = [pltpu.make_async_copy(weights[i], held[i], sems.at[i]) for i in range(6)]
    for copy in copies:
        copy.start()
    x = jnp.concatenate([near_rows[...], far_rows[...]], axis=0)
    sent = []
    for half in range(2):
        gate_copy, up_copy, down_copy = copies[3 * half : 3 * half + 3]
        gate_half, up_half, down_half = held[3 * half : 3 * half + 3]
        gate_copy.wait()
        gate = jnp.dot(x, gate_half[...], preferred_element_type=jnp.float32)
        up_copy.wait()
        up = jnp.dot(x, up_half[...], preferred_element_type=jnp.float32)
        activation = (gate / (1.0 + jnp.exp(-gate)) * up).astype(jnp.bfloat16)
        down_copy.wait()
        for i, start in enumerate(range(0, width, STEP)):
            cut = pl.ds(start, STEP)
            partial = jnp.dot(
                activation, down_half[:, cut], preferred_element_type=jnp.float32
            ).astype(jnp.bfloat16)
            if half == 0:
                total[:, cut] = partial
                continue
            sums = total[:, cut].astype(jnp.float32) + partial.astype(jnp.float32)
            for j, (built, out) in enumerate(((near_built, near), (far_built, far))):
                built[:, cut] = sums[j * count : (j + 1) * count].astype(jnp.bfloat16)
                sent.append(
                    pltpu.make_async_copy(built.at[:, cut], out.at[:, cut], out_sems.at[j, i])
                )
                sent[-1].start()
    for copy in sent:
        copy.wait()


def experts(near_rows, far_rows, weights):
    half, kind = near_rows.shape, near_rows.dtype
    count, width = 2 * half[0], half[1]
    hbm = pl.BlockSpec(memory_space=pltpu.HBM)
    return pl.pallas_call(
        expert_kernel,
        out_shape=[pltpu.HBM(half, kind)] * 2,
        in_specs=[pl.BlockSpec(memory_space=pltpu.VMEM)] * 2 + [hbm] * 6,
        out_specs=[hbm] * 2,
        scratch_shapes=[pltpu.VMEM(w.shape, w.dtype) for w in weights]
        + [pltpu.VMEM(half, kind)] * 2
        + [
            pltpu.VMEM((count, width), kind),
            pltpu.SemaphoreType.DMA((6,)),
            pltpu.SemaphoreType.DMA((2, width // STEP)),
        ],
        compiler_params=pltpu.CompilerParams(vmem_limit_bytes=40 * MIB),
        cost_estimate=pl.CostEstimate(
            flops=2 * count * sum(w.size for w in weights),
            bytes_accessed=2 * sum(w.size for w in weights),
            transcendentals=0,
        ),
    )(near_rows, far_rows, *(in_hbm(w) for w in weights))


def from_line(rows, distance):
    planes = lax.axis_size("z")
    return lax.ppermute(rows, "z", [((i + distance) % planes, i) for i in range(planes)])


def per_device(
    tokens,
    norm_gain,
    routes,
    route_weight,
    w_gate,
    w_up,
    w_down,
    query_latent,
    query_rope,
    cache_latent,
    cache_rope,
    lengths,
):
    planes = lax.axis_size("z")
    places = lax.axis_size(PLANE)
    count, top = routes.shape
    width = tokens.shape[1]
    blocks = planes // 2
    slots = 2 * blocks
    rows = places * slots
    f32 = jnp.float32

    def to_plane(x):
        return lax.all_to_all(x, PLANE, split_axis=0, concat_axis=0, tiled=True)

    packed = normalize(tokens, norm_gain, routes, route_weight)
    weights = (w_gate[0], w_up[0], w_down[0])

    up2, down2 = from_line(packed, 2), from_line(packed, -2)
    up1, down1 = from_line(packed, 1), from_line(packed, -1)
    (up2, down2, up1, down1), held = lax.optimization_barrier(
        ((up2, down2, up1, down1), weights[1:])
    )
    across, up3, down3 = from_line(up2, 2), from_line(up2, 1), from_line(down2, -1)
    far_weights = [lax.ppermute(w, "c", [(0, 1), (1, 0)]) for w in (weights[0], *held)]

    own = (
        (jnp.arange(rows, dtype=jnp.int32) // slots) * planes + lax.axis_index("z")
    ).astype(f32)[None]
    near, near_scale = dispatch(top, width, own, packed, up1, up2, down2)
    far, far_scale = dispatch(top, width, own, down1, up3, across, down3)
    near_rows = to_plane(near)
    near_rows, far = lax.optimization_barrier((near_rows, far))
    far_rows = to_plane(far)
    near_result, far_result = experts(near_rows, far_rows, (*weights, *far_weights))
    far_back = to_plane(far_result)
    attended = attention(query_latent, query_rope, cache_latent, cache_rope, lengths)
    far_back, near_result = lax.optimization_barrier((far_back, near_result))
    near_back = to_plane(near_result)
    flops = 4 * rows * count * blocks * width
    down1, up3, across, down3 = call(
        far_kernel,
        (shape(count, width),) * 4,
        far_scale,
        far_back,
        limit=8,
        flops=flops,
    )
    across, up3, down3 = from_line(across, -2), from_line(up3, -1), from_line(down3, 1)
    down1 = from_line(down1, 1)
    up3, across, down3, attended = lax.optimization_barrier((up3, across, down3, attended))
    own_sum, up1, up2, down2 = call(
        near_kernel,
        (shape(count, width, dtype=f32),) + (shape(count, width),) * 3,
        near_scale,
        near_back,
        up3,
        across,
        down3,
        limit=8,
        flops=flops,
    )
    up2, down2, up1 = from_line(up2, -2), from_line(down2, 2), from_line(up1, -1)
    layer_out = call(
        final_kernel, shape(count, width), tokens, own_sum, up2, down2, up1, down1, limit=4
    )
    return layer_out, attended


def solution(mesh):
    split = Mesh(mesh.devices.reshape(2, 4, 2, 8, 2), ALL)
    return jax.shard_map(
        per_device,
        mesh=split,
        in_specs=(
            P(ALL, None),
            P(),
            P(ALL, None),
            P(ALL, None),
            P(EXPERT, None, "c"),
            P(EXPERT, None, "c"),
            P(EXPERT, "c", None),
            P(ALL, None, None),
            P(ALL, None, None),
            P(ALL, None, None),
            P(ALL, None, None),
            P(ALL),
        ),
        out_specs=(P(ALL, None), P(ALL, None, None)),
        check_vma=False,
    )
```

```python
import functools
import jax
import jax.numpy as jnp
from jax import lax
from jax.experimental import pallas as pl
from jax.experimental.pallas import tpu as pltpu
from jax.sharding import Mesh, PartitionSpec as P

score_scale = 192.0 ** (-0.5)
epsilon = 1e-06
PLANE = ("xl", "y", "xh")
EXPERT = ("xl", "y", "xh", "z")
ALL = ("xl", "y", "xh", "z", "c")
TAIL = 128
STEP = 512
MIB = 1024 * 1024


def attention_kernel(lengths, latent_in, rope_in, cache_in, cache_rope_in, out, *scratch):
    latent, rope, cache, cache_rope, built, sems, out_sems = scratch
    requests, positions = cache.shape[0], cache.shape[1]
    sources = (cache_in, latent_in, cache_rope_in, rope_in)
    targets = (cache, latent, cache_rope, rope)
    copies = [
        [
            pltpu.make_async_copy(source.at[r], target.at[r], sems.at[i, r])
            for i, (source, target) in enumerate(zip(sources, targets))
        ]
        for r in range(requests)
    ]
    for group in copies:
        for copy in group:
            copy.start()
    scores, sent = [], []
    for r in range(requests):
        for copy in copies[r]:
            copy.wait()
        score = lax.dot_general(
            latent[r], cache[r], (((1,), (1,)), ((), ())), preferred_element_type=jnp.float32
        )
        score = (
            score
            + lax.dot_general(
                rope[r], cache_rope[r], (((0,), (0,)), ((), ())), preferred_element_type=jnp.float32
            )
        ) * score_scale
        position = lax.broadcasted_iota(jnp.int32, score.shape, 1)
        scores.append(jnp.where(position < lengths[r], score, -1e30))
    weights = [jnp.exp(score - jnp.max(score, axis=1, keepdims=True)) for score in scores]
    probabilities = [
        (weight / jnp.sum(weight, axis=1, keepdims=True)).astype(jnp.bfloat16)
        for weight in weights
    ]
    for r in range(requests):
        built[r] = jnp.dot(
            probabilities[r], cache[r], preferred_element_type=jnp.float32
        ).astype(jnp.bfloat16)
        sent.append(pltpu.make_async_copy(built.at[r], out.at[r], out_sems.at[r]))
        sent[-1].start()
    for copy in sent:
        copy.wait()


def attention(query_latent, query_rope, cache_latent, cache_rope, lengths):
    operands = (query_latent, jnp.swapaxes(query_rope, 1, 2), cache_latent, cache_rope)
    requests = lengths.shape[0]
    hbm = pl.BlockSpec(memory_space=pltpu.HBM)
    return pl.pallas_call(
        attention_kernel,
        out_shape=pltpu.HBM(query_latent.shape, query_latent.dtype),
        in_specs=[pl.BlockSpec(memory_space=pltpu.SMEM)] + [hbm] * 4,
        out_specs=hbm,
        scratch_shapes=[pltpu.VMEM(x.shape, x.dtype) for x in operands]
        + [
            pltpu.VMEM(query_latent.shape, query_latent.dtype),
            pltpu.SemaphoreType.DMA((4, requests)),
            pltpu.SemaphoreType.DMA((requests,)),
        ],
        compiler_params=pltpu.CompilerParams(vmem_limit_bytes=12 * MIB),
        cost_estimate=pl.CostEstimate(
            flops=4 * cache_latent.size * query_latent.shape[1],
            bytes_accessed=4 * cache_latent.size,
            transcendentals=0,
        ),
    )(lengths, *(in_hbm(x) for x in operands))


def call(kernel, out_shape, *operands, limit, flops=0, scratch=()):
    moved = sum(x.size * x.dtype.itemsize for x in operands) + sum(
        x.size * x.dtype.itemsize for x in jax.tree.leaves(out_shape)
    )
    return pl.pallas_call(
        kernel,
        out_shape=out_shape,
        scratch_shapes=scratch,
        compiler_params=pltpu.CompilerParams(vmem_limit_bytes=limit * MIB),
        cost_estimate=pl.CostEstimate(flops=flops, bytes_accessed=moved, transcendentals=0),
    )(*operands)


def shape(*dims, dtype=jnp.bfloat16):
    return jax.ShapeDtypeStruct(dims, dtype)


def in_hbm(x):
    return pltpu.with_memory_space_constraint(x, pltpu.HBM)


def norm_kernel(tokens_in, gain_in, routes_in, weight_in, packed, tokens, gain, routes, route_weight, sems):
    copies = [
        pltpu.make_async_copy(source, target, sems.at[i])
        for i, (source, target) in enumerate(
            (
                (routes_in, routes),
                (weight_in, route_weight),
                (tokens_in, tokens),
                (gain_in, gain.at[0]),
            )
        )
    ]
    for copy in copies:
        copy.start()
    width = tokens.shape[1]
    top = routes.shape[0]
    copies[0].wait()
    copies[1].wait()
    weight = route_weight[...]
    high = weight.astype(jnp.bfloat16).astype(jnp.float32)
    middle = (weight - high).astype(jnp.bfloat16).astype(jnp.float32)
    low = weight - high - middle
    columns = jnp.concatenate([routes[...].astype(jnp.float32), high, middle, low], axis=0)
    row = lax.broadcasted_iota(jnp.int32, (4 * top, TAIL), 0)
    column = lax.broadcasted_iota(jnp.int32, (4 * top, TAIL), 1)
    unit = jnp.where(row == column, 1.0, 0.0).astype(jnp.bfloat16)
    packed[:, width:] = lax.dot_general(
        columns.astype(jnp.bfloat16),
        unit,
        (((0,), (0,)), ((), ())),
        preferred_element_type=jnp.float32,
    ).astype(jnp.bfloat16)
    copies[2].wait()
    widened = tokens[...].astype(jnp.float32)
    inverse = lax.rsqrt(jnp.mean(widened * widened, axis=1, keepdims=True) + epsilon)
    copies[3].wait()
    packed[:, :width] = (widened * inverse * gain[...]).astype(jnp.bfloat16)


def normalize(tokens, gain, routes, route_weight):
    operands = (tokens, gain, routes.T, route_weight.T)
    return pl.pallas_call(
        norm_kernel,
        out_shape=shape(tokens.shape[0], tokens.shape[1] + TAIL),
        in_specs=[pl.BlockSpec(memory_space=pltpu.HBM)] * 4,
        scratch_shapes=[
            pltpu.VMEM(tokens.shape, tokens.dtype),
            pltpu.VMEM((1,) + gain.shape, gain.dtype),
            pltpu.VMEM(operands[2].shape, routes.dtype),
            pltpu.VMEM(operands[3].shape, route_weight.dtype),
            pltpu.SemaphoreType.DMA((4,)),
        ],
        compiler_params=pltpu.CompilerParams(vmem_limit_bytes=4 * MIB),
        cost_estimate=pl.CostEstimate(
            flops=4 * tokens.size, bytes_accessed=4 * tokens.size, transcendentals=0
        ),
    )(*(in_hbm(x) for x in operands))


def slots_of(info, experts, count, top):
    gathered, places = info.shape[0], experts.shape[1]
    names = info[:, 0:1] == experts
    for k in range(1, top):
        names = names | (info[:, k : k + 1] == experts)
    row = lax.broadcasted_iota(jnp.int32, (gathered, gathered), 0)
    column = lax.broadcasted_iota(jnp.int32, (gathered, gathered), 1)
    before = jnp.where((column < row) & (column // count == row // count), 1.0, 0.0)
    rank = jnp.dot(
        before.astype(jnp.bfloat16),
        jnp.where(names, 1.0, 0.0).astype(jnp.bfloat16),
        preferred_element_type=jnp.float32,
    )
    token = lax.broadcasted_iota(jnp.int32, (gathered, places), 0)
    slot = lax.broadcasted_iota(jnp.int32, (gathered, places), 1) % (2 * gathered // count)
    return names & ((token // count) * 2 + rank.astype(jnp.int32) == slot)


def weights_of(info, experts, top):
    weight = jnp.zeros((info.shape[0], experts.shape[1]), jnp.float32)
    shares = (
        info[:, top : 2 * top] + info[:, 2 * top : 3 * top] + info[:, 3 * top : 4 * top]
    )
    for k in range(top):
        weight = weight + jnp.where(
            info[:, k : k + 1] == experts, shares[:, k : k + 1], 0.0
        )
    return weight


def dispatch_kernel(top, own, *refs):
    blocks, (outgoing, scale, built, sems) = refs[:-4], refs[-4:]
    count = blocks[0].shape[0]
    width = outgoing.shape[1]
    info = jnp.concatenate([b[:, width:] for b in blocks], axis=0).astype(jnp.float32)
    here = slots_of(info, own[...], count, top)
    place = jnp.where(here, 1.0, 0.0).astype(jnp.bfloat16)
    copies = []
    for i, start in enumerate(range(0, width, STEP)):
        cut = pl.ds(start, STEP)
        rows = jnp.concatenate([b[:, start : start + STEP] for b in blocks], axis=0)
        built[:, cut] = lax.dot_general(
            place, rows, (((0,), (0,)), ((), ())), preferred_element_type=jnp.float32
        ).astype(jnp.bfloat16)
        copies.append(pltpu.make_async_copy(built.at[:, cut], outgoing.at[:, cut], sems.at[i]))
        copies[-1].start()
    scale[...] = jnp.where(here, weights_of(info, own[...], top), 0.0)
    for copy in copies:
        copy.wait()


def dispatch(top, width, own, *blocks):
    gathered, rows = blocks[0].shape[0] * len(blocks), own.shape[1]
    return pl.pallas_call(
        functools.partial(dispatch_kernel, top),
        out_shape=[
            pltpu.HBM((rows, width), jnp.bfloat16),
            shape(gathered, rows, dtype=jnp.float32),
        ],
        out_specs=[pl.BlockSpec(memory_space=pltpu.HBM), pl.BlockSpec(memory_space=pltpu.VMEM)],
        scratch_shapes=[
            pltpu.VMEM((rows, width), jnp.bfloat16),
            pltpu.SemaphoreType.DMA((width // STEP,)),
        ],
        compiler_params=pltpu.CompilerParams(vmem_limit_bytes=8 * MIB),
        cost_estimate=pl.CostEstimate(
            flops=2 * rows * gathered * width,
            bytes_accessed=4 * rows * width,
            transcendentals=0,
        ),
    )(own, *blocks)


def weighted(scale, rows):
    high = scale.astype(jnp.bfloat16)
    low = (scale - high.astype(jnp.float32)).astype(jnp.bfloat16)
    return jnp.dot(high, rows, preferred_element_type=jnp.float32) + jnp.dot(
        low, rows, preferred_element_type=jnp.float32
    )


def far_kernel(scale, returned, *blocks):
    count, width = blocks[0].shape
    step = 512
    for start in range(0, width, step):
        cut = slice(start, start + step)
        sums = weighted(scale[...], returned[:, cut])
        for i, block in enumerate(blocks):
            block[:, cut] = sums[i * count : (i + 1) * count].astype(block.dtype)


def near_kernel(scale, returned, up3, across, down3, own, up1, up2, down2):
    count, width = own.shape
    f32 = jnp.float32
    for start in range(0, width, STEP):
        cut = slice(start, start + STEP)
        sums = weighted(scale[...], returned[:, cut])
        own[:, cut] = sums[:count]
        up1[:, cut] = sums[count : 2 * count].astype(jnp.bfloat16)
        up2[:, cut] = (
            sums[2 * count : 3 * count] + up3[:, cut].astype(f32) + across[:, cut].astype(f32)
        ).astype(jnp.bfloat16)
        down2[:, cut] = (sums[3 * count :] + down3[:, cut].astype(f32)).astype(jnp.bfloat16)


def final_kernel(tokens, own, *refs):
    total = own[...]
    for part in refs[:-1]:
        total = total + part[...].astype(jnp.float32)
    refs[-1][...] = (tokens[...].astype(jnp.float32) + total).astype(jnp.bfloat16)


def expert_kernel(near_rows, far_rows, *refs):
    weights, (near, far), held = refs[:6], refs[6:8], refs[8:14]
    near_built, far_built, total, sems, out_sems = refs[14:]
    count, width = near.shape
    copies = [pltpu.make_async_copy(weights[i], held[i], sems.at[i]) for i in range(6)]
    for copy in copies:
        copy.start()
    x = jnp.concatenate([near_rows[...], far_rows[...]], axis=0)
    sent = []
    for half in range(2):
        gate_copy, up_copy, down_copy = copies[3 * half : 3 * half + 3]
        gate_half, up_half, down_half = held[3 * half : 3 * half + 3]
        gate_copy.wait()
        gate = jnp.dot(x, gate_half[...], preferred_element_type=jnp.float32)
        up_copy.wait()
        up = jnp.dot(x, up_half[...], preferred_element_type=jnp.float32)
        activation = (gate / (1.0 + jnp.exp(-gate)) * up).astype(jnp.bfloat16)
        down_copy.wait()
        for i, start in enumerate(range(0, width, STEP)):
            cut = pl.ds(start, STEP)
            partial = jnp.dot(
                activation, down_half[:, cut], preferred_element_type=jnp.float32
            ).astype(jnp.bfloat16)
            if half == 0:
                total[:, cut] = partial
                continue
            sums = total[:, cut].astype(jnp.float32) + partial.astype(jnp.float32)
            for j, (built, out) in enumerate(((near_built, near), (far_built, far))):
                built[:, cut] = sums[j * count : (j + 1) * count].astype(jnp.bfloat16)
                sent.append(
                    pltpu.make_async_copy(built.at[:, cut], out.at[:, cut], out_sems.at[j, i])
                )
                sent[-1].start()
    for copy in sent:
        copy.wait()


def experts(near_rows, far_rows, weights):
    half, kind = near_rows.shape, near_rows.dtype
    count, width = 2 * half[0], half[1]
    hbm = pl.BlockSpec(memory_space=pltpu.HBM)
    return pl.pallas_call(
        expert_kernel,
        out_shape=[pltpu.HBM(half, kind)] * 2,
        in_specs=[pl.BlockSpec(memory_space=pltpu.VMEM)] * 2 + [hbm] * 6,
        out_specs=[hbm] * 2,
        scratch_shapes=[pltpu.VMEM(w.shape, w.dtype) for w in weights]
        + [pltpu.VMEM(half, kind)] * 2
        + [
            pltpu.VMEM((count, width), kind),
            pltpu.SemaphoreType.DMA((6,)),
            pltpu.SemaphoreType.DMA((2, width // STEP)),
        ],
        compiler_params=pltpu.CompilerParams(vmem_limit_bytes=40 * MIB),
        cost_estimate=pl.CostEstimate(
            flops=2 * count * sum(w.size for w in weights),
            bytes_accessed=2 * sum(w.size for w in weights),
            transcendentals=0,
        ),
    )(near_rows, far_rows, *(in_hbm(w) for w in weights))


def from_line(rows, distance):
    planes = lax.axis_size("z")
    return lax.ppermute(rows, "z", [((i + distance) % planes, i) for i in range(planes)])


def per_device(
    tokens,
    norm_gain,
    routes,
    route_weight,
    w_gate,
    w_up,
    w_down,
    query_latent,
    query_rope,
    cache_latent,
    cache_rope,
    lengths,
):
    planes = lax.axis_size("z")
    places = lax.axis_size(PLANE)
    count, top = routes.shape
    width = tokens.shape[1]
    blocks = planes // 2
    slots = 2 * blocks
    rows = places * slots
    f32 = jnp.float32

    def to_plane(x):
        return lax.all_to_all(x, PLANE, split_axis=0, concat_axis=0, tiled=True)

    packed = normalize(tokens, norm_gain, routes, route_weight)
    weights = (w_gate[0], w_up[0], w_down[0])

    up2, down2 = from_line(packed, 2), from_line(packed, -2)
    up1, down1 = from_line(packed, 1), from_line(packed, -1)
    (up2, down2, up1, down1), held = lax.optimization_barrier(
        ((up2, down2, up1, down1), weights[1:])
    )
    across, up3, down3 = from_line(up2, 2), from_line(up2, 1), from_line(down2, -1)
    far_weights = [lax.ppermute(w, "c", [(0, 1), (1, 0)]) for w in (weights[0], *held)]

    own = (
        (jnp.arange(rows, dtype=jnp.int32) // slots) * planes + lax.axis_index("z")
    ).astype(f32)[None]
    near, near_scale = dispatch(top, width, own, packed, up1, up2, down2)
    far, far_scale = dispatch(top, width, own, down1, up3, across, down3)
    near_rows = to_plane(near)
    near_rows, far = lax.optimization_barrier((near_rows, far))
    far_rows = to_plane(far)
    near_result, far_result = experts(near_rows, far_rows, (*weights, *far_weights))
    far_back = to_plane(far_result)
    attended = attention(query_latent, query_rope, cache_latent, cache_rope, lengths)
    far_back, near_result = lax.optimization_barrier((far_back, near_result))
    near_back = to_plane(near_result)
    flops = 4 * rows * count * blocks * width
    down1, up3, across, down3 = call(
        far_kernel,
        (shape(count, width),) * 4,
        far_scale,
        far_back,
        limit=8,
        flops=flops,
    )
    across, up3, down3 = from_line(across, -2), from_line(up3, -1), from_line(down3, 1)
    down1 = from_line(down1, 1)
    up3, across, down3, attended = lax.optimization_barrier((up3, across, down3, attended))
    own_sum, up1, up2, down2 = call(
        near_kernel,
        (shape(count, width, dtype=f32),) + (shape(count, width),) * 3,
        near_scale,
        near_back,
        up3,
        across,
        down3,
        limit=8,
        flops=flops,
    )
    up2, down2, up1 = from_line(up2, -2), from_line(down2, 2), from_line(up1, -1)
    layer_out = call(
        final_kernel, shape(count, width), tokens, own_sum, up2, down2, up1, down1, limit=4
    )
    return layer_out, attended


def solution(mesh):
    split = Mesh(mesh.devices.reshape(2, 4, 2, 8, 2), ALL)
    return jax.shard_map(
        per_device,
        mesh=split,
        in_specs=(
            P(ALL, None),
            P(),
            P(ALL, None),
            P(ALL, None),
            P(EXPERT, None, "c"),
            P(EXPERT, None, "c"),
            P(EXPERT, "c", None),
            P(ALL, None, None),
            P(ALL, None, None),
            P(ALL, None, None),
            P(ALL, None, None),
            P(ALL),
        ),
        out_specs=(P(ALL, None), P(ALL, None, None)),
        check_vma=False,
    )
```
